512 devices in a mesh: seq: 16 (over x, y_hi, core), expert: 32 (over z, y_lo).
Axes of the slice: x: 4, y: 4 (y_hi: 2, y_lo: 2; y = y_hi * 2 + y_lo), z: 16, core: 2. Of those that a mesh axis runs over, the one named last changes fastest.
Arguments:
- tokens: bfloat16 [8192, 1024], P('seq', 'expert'), may hold values from -128 to 128
- mix: bfloat16 [1024, 4096], P(None, 'expert'), may hold values from -2 to 2
- w_in: bfloat16 [64, 1024, 4096], P('expert', None, 'seq'), may hold values from -0.5 to 0.5
- w_out: bfloat16 [64, 4096, 1024], P('expert', 'seq'), may hold values from -0.25 to 0.25
- cotangent: bfloat16 [8192, 1024], P('seq', 'expert'), may hold values from -6 to 6
Outputs:
- mixed: bfloat16 [8192, 1024], P('seq', 'expert')
- grad_tokens: bfloat16 [8192, 1024], P('seq', 'expert')
- grad_mix: bfloat16 [1024, 4096], P(None, 'expert')
- grad_w_in: bfloat16 [64, 1024, 4096], P('expert', None, 'seq')
- grad_w_out: bfloat16 [64, 4096, 1024], P('expert', 'seq')
The draws below stay inside these ranges and needn't reach their ends.
All inputs are finite; a program needn't handle non-finite values.
Results may differ from the reference program's by a relative error of at most 0.027.
Values may be sent and summed in bfloat16 or wider, within the bound.
A program may use at most 64 MiB of HBM per device.

```python
import math
import jax
import jax.numpy as jnp
from jax import lax

D = 1024
H = 4096
S = 64
EXP_DEV = 2
EXPERTS = 64
SLOTS = 4096
TOKENS = 8192
N_EXPERT = 32


def mix_table(key):
    base = jnp.clip(jax.random.normal(jax.random.fold_in(key, 101), (D, SLOTS), jnp.float32), -4.0, 4.0)
    ramp = 1.0 + 0.25 * jnp.arange(SLOTS, dtype=jnp.float32) / max(SLOTS - 1, 1)
    table = base * ramp[None, :] * (2.2 / math.sqrt(D))
    return lax.optimization_barrier(table.astype(jnp.bfloat16)).astype(jnp.float32)


def draw_mix(key, part):
    table = mix_table(key)
    return table.astype(jnp.bfloat16)


def draw_tokens(key, part):
    key = jax.random.fold_in(key, 2)
    keys = jax.random.split(key, 1)
    ramp = 1.0 + 0.25 * jnp.arange(TOKENS, dtype=jnp.float32) / max(TOKENS - 1, 1)
    values = jnp.clip(jax.random.normal(keys[0], (TOKENS, D), jnp.float32), -5.0, 5.0) * ramp[:, None]
    return values.astype(jnp.bfloat16)


def shard_levels(key, dims, pieces, least, largest):
    factor_of = 1.0
    for axis_at, blocks in pieces:
        steps = jax.random.uniform(jax.random.fold_in(jax.random.fold_in(key, 6), axis_at), (blocks,), jnp.float32, least / len(pieces), largest / len(pieces))
        factor_of = factor_of * jnp.repeat(jnp.exp(steps), dims[axis_at] // blocks).reshape((-1,) + (1,) * (len(dims) - 1 - axis_at))
    return factor_of


def normal_values(key, shape, spread, bound, shards=(), held_as=jnp.bfloat16):
    entries = spread * jax.random.normal(key, shape, jnp.float32)
    if shards:
        entries = entries * shard_levels(key, shape, shards, -0.22, 0.18)
    return jnp.clip(entries, -bound, bound).astype(held_as)


def setup_inputs(seed: int = 0) -> dict:
    streams_of = jax.random.split(jax.random.key(seed), 6)
    return {
        "tokens": draw_tokens(jax.random.fold_in(streams_of[5], 71), 0),
        "mix": draw_mix(jax.random.fold_in(streams_of[5], 71), 0),
        "w_in": normal_values(streams_of[2], (EXPERTS, D, H), (D // 9) ** -0.5, 0.5, ((0, 32), (2, 16))),
        "w_out": normal_values(streams_of[3], (EXPERTS, H, D), (H // 9) ** -0.5, 0.25, ((0, 32), (1, 16))),
        "cotangent": normal_values(streams_of[4], (TOKENS, D), 1.0, 6.0, ((0, 16), (1, 32))),
    }


def softmax_axis(values, axis):
    peak = lax.optimization_barrier(jnp.max(values, axis=axis, keepdims=True))
    scaled = jnp.exp(values - peak)
    return scaled / lax.optimization_barrier(jnp.sum(scaled, axis=axis, keepdims=True))

def grouped_sum(pairs):
    span = EXP_DEV * S
    rows = pairs[0][0].shape[0]
    width = pairs[0][1].shape[1]

    def step(total, group):
        start = (group * span).astype(jnp.int32)
        term = jnp.zeros((rows, width), jnp.float32)
        for left, right in pairs:
            left_part = lax.dynamic_slice_in_dim(left, start, span, 1)
            right_part = lax.dynamic_slice_in_dim(right, start, span, 0)
            term = term + jnp.dot(left_part, right_part, preferred_element_type=jnp.float32)
        rounded = lax.optimization_barrier(term.astype(jnp.bfloat16)).astype(jnp.float32)
        return (total + rounded, None)
    groups = jnp.arange(N_EXPERT, dtype=jnp.int32)
    total, _ = lax.scan(step, jnp.zeros((rows, width), jnp.float32), groups)
    return total.astype(jnp.bfloat16)

def expert_forward(operands):
    slot_rows, first, second = operands
    pre = jnp.dot(slot_rows, first, preferred_element_type=jnp.float32)
    act = jax.nn.gelu(pre).astype(jnp.bfloat16)
    out = jnp.dot(act, second, preferred_element_type=jnp.float32).astype(jnp.bfloat16)
    return (pre, act, out)

def expert_backward(operands):
    slot_rows, first, second, pre, act, grad_rows = operands
    grad_second = jnp.dot(act.T, grad_rows, preferred_element_type=jnp.float32).astype(jnp.bfloat16)
    d_act = jnp.dot(grad_rows, second.T, preferred_element_type=jnp.float32)
    _, pull = jax.vjp(jax.nn.gelu, pre)
    d_pre = pull(d_act)[0].astype(jnp.bfloat16)
    grad_first = jnp.dot(slot_rows.T, d_pre, preferred_element_type=jnp.float32).astype(jnp.bfloat16)
    d_rows = jnp.dot(d_pre, first.T, preferred_element_type=jnp.float32).astype(jnp.bfloat16)
    return (grad_first, grad_second, d_rows)

def reference(tokens, mix, w_in, w_out, cotangent):
    logits = jnp.dot(tokens, mix, preferred_element_type=jnp.float32)
    dispatch = softmax_axis(logits, 0)
    dispatch_b = dispatch.astype(jnp.bfloat16)
    slot_in = jnp.dot(dispatch_b.T, tokens, preferred_element_type=jnp.float32).astype(jnp.bfloat16)
    grouped_in = slot_in.reshape(EXPERTS, S, D)
    pre, act, grouped_out = lax.map(expert_forward, (grouped_in, w_in, w_out))
    slot_out = grouped_out.reshape(SLOTS, D)
    combine = softmax_axis(logits, 1)
    combine_b = combine.astype(jnp.bfloat16)
    mixed = grouped_sum([(combine_b, slot_out)])
    d_comb = jnp.dot(cotangent, slot_out.T, preferred_element_type=jnp.float32)
    row_sum = lax.optimization_barrier(jnp.sum(combine * d_comb, axis=1, keepdims=True))
    d_logit_comb = combine * (d_comb - row_sum)
    d_slot_out = jnp.dot(combine_b.T, cotangent, preferred_element_type=jnp.float32).astype(jnp.bfloat16)
    grad_w_in, grad_w_out, d_grouped = lax.map(expert_backward, (grouped_in, w_in, w_out, pre, act, d_slot_out.reshape(EXPERTS, S, D)))
    d_slot_in = d_grouped.reshape(SLOTS, D)
    d_disp = jnp.dot(tokens, d_slot_in.T, preferred_element_type=jnp.float32)
    col_sum = lax.optimization_barrier(jnp.sum(dispatch * d_disp, axis=0, keepdims=True))
    d_logit = (dispatch * (d_disp - col_sum) + d_logit_comb).astype(jnp.bfloat16)
    grad_mix = jnp.dot(tokens.T, d_logit, preferred_element_type=jnp.float32).astype(jnp.bfloat16)
    grad_tokens = grouped_sum([(dispatch_b, d_slot_in), (d_logit, mix.T)])
    return (mixed, grad_tokens, grad_mix, grad_w_in, grad_w_out)
```

```python
import functools
import math

import jax
import jax.numpy as jnp
from jax import lax
from jax.experimental import pallas as pl
from jax.experimental.pallas import tpu as pltpu
from jax.sharding import PartitionSpec as P

MESH = pl.DeviceIdType.MESH
F32 = jnp.float32
BF = jnp.bfloat16
GELU_K = math.sqrt(2.0 / math.pi)

D = 1024
TOK = 256
SLOT = 256
OWN = 128
HID = 256
HALF = 512

(Z_TOK1, Z_TOK2, Z_COT1, Z_COT2, ROWST, COLST, ROWSUM, COLSUM, MIXX,
 X_SI, R_SI, A_SI, F_SI, X_DO, R_DO, A_DO, F_DO, X_SO, R_SO, A_SO, F_SO,
 X_DI, R_DI, A_DI, F_DI, X_GM, R_GM, A_GM, F_GM,
 ZM1, ZM2, ZG1, ZG2, NSEM) = range(34)
(L_TOK, L_COT, L_MIX, L_WI, L_WO, L_GWI, L_GWO, L_MX, L_GT, L_GM, NLOC) = range(11)


def dot(a, b):
    return jnp.dot(a, b, preferred_element_type=F32)


def kernel(tok_h, mix_h, win_h, wout_h, cot_h,
           mixed_o, gtok_o, gmix_o, gwin_o, gwout_o,
           tokv, cotv, tt, ct, tn, cn, mh, mt, wi, wo, wit, wot,
           rowst, colst, rowb, colb, rsum, csum, rsumb, csumb,
           pb, xb, sb, rb, ab, pb2, xb2, sb2, rb2, ab2,
           pz, rz, sz, fz, lt, disp, dispb, combt, combb, dcomb, ddisp, dlog, part1,
           prev, actv, dprev, gwi, gwo, outv, gmv, seven,
           ss, rs, ls):
    s = lax.axis_index("seq")
    e = lax.axis_index("expert")
    u, c = s // 2, s % 2
    z, yl = e // 2, e % 2
    zh, zl = z // 4, z % 4
    r = yl * 8 + u
    p = r * 2 + c

    def dev(u_, yl_, z_, c_):
        return (u_ * 2 + c_, z_ * 2 + yl_)

    def chip(r_, c_):
        return dev(r_ % 8, r_ // 8, z, c_)

    def send(src, dst, k, to, rk=None):
        pltpu.make_async_remote_copy(
            src_ref=src, dst_ref=dst, send_sem=ss.at[k], recv_sem=rs.at[k if rk is None else rk],
            device_id=to, device_id_type=MESH).start()

    def wait(ref, sem):
        pltpu.make_async_copy(ref, ref, sem).wait()

    def wait_recv(ref, k):
        wait(ref, rs.at[k])

    def wait_send(ref, k):
        wait(ref, ss.at[k])

    def local(src, dst, k):
        cp = pltpu.make_async_copy(src, dst, ls.at[k])
        cp.start()
        return cp

    def each(n, f):
        def body(i, carry):
            f(i)
            return carry
        lax.fori_loop(0, n, body, 0)

    for h in range(2):
        local(tok_h.at[:, pl.ds(h * TOK, TOK)], tokv.at[h], L_TOK)
    for h in range(2):
        local(cot_h.at[:, pl.ds(h * TOK, TOK)], cotv.at[h], L_COT)
    local(mix_h, mh.at[yl], L_MIX)
    local(win_h, wi, L_WI)
    local(wout_h, wo, L_WO)

    bar = pltpu.get_barrier_semaphore()

    def sig(to):
        pl.semaphore_signal(bar, inc=1, device_id=to, device_id_type=MESH)

    def sig_plane(i):
        q = (p + 1 + i) % 32
        sig(chip(q // 2, q % 2))
    each(31, sig_plane)
    each(15, lambda i: sig(dev(u, yl, (z + 1 + i) % 16, c)))
    each(3, lambda i: sig(dev(u, 1 - yl, (z + 4 * (i + 1)) % 16, c)))
    pl.semaphore_wait(bar, 49)

    def gather1(src, dst, k):
        def one(i):
            zz = (z + 4 * (i // 2)) % 16
            yy = (yl + i % 2) % 2
            send(src.at[yy], dst.at[zh, zl, yl], k, dev(u, yy, zz, c))

        def step(i):
            one(i + 1)
        each(7, step)
        dst[zh, zl, yl] = src[yl]

    def gather2(buf, k1, k2):
        wait_recv(seven, k1)
        send(buf.at[:, zl], buf.at[:, zl], k2, dev(u, yl, (z + 1) % 16, c))
        send(buf.at[:, zl], buf.at[:, zl], k2, dev(u, yl, (z + 15) % 16, c))
        send(buf.at[pl.ds(0, 2), zl], buf.at[pl.ds(0, 2), zl], k2, dev(u, yl, (z + 2) % 16, c))
        send(buf.at[pl.ds(2, 2), zl], buf.at[pl.ds(2, 2), zl], k2, dev(u, yl, (z + 14) % 16, c))

    wait(tokv, ls.at[L_TOK])
    gather1(tokv, tt, Z_TOK1)
    wait(mh.at[0], ls.at[L_MIX])
    send(mh.at[yl], mh.at[yl], MIXX, dev(u, 1 - yl, z, c))
    mt[pl.ds(pl.multiple_of(yl * OWN, OWN), OWN), :] = mh[yl].T
    wait(cotv, ls.at[L_COT])
    gather2(tt, Z_TOK1, Z_TOK2)
    gather1(cotv, ct, Z_COT1)
    wait_recv(mh.at[0], MIXX)
    mt[pl.ds(pl.multiple_of((1 - yl) * OWN, OWN), OWN), :] = mh[1 - yl].T
    wait(wi, ls.at[L_WI])
    wait(wo, ls.at[L_WO])
    for k in range(2):
        wit[k] = wi[k].T
        wot[k] = wo[k].T
    wait_recv(tt.at[:, pl.ds(0, 3)], Z_TOK2)

    ttv = tt[...].reshape(D, TOK)
    logits = dot(mt[...], ttv)
    lt[...] = logits
    rm = jnp.max(logits, axis=0, keepdims=True)
    rsm = jnp.sum(jnp.exp(logits - rm), axis=0, keepdims=True)

    def put(ref, at, v):
        ref[at:at + 1, :] = v[:, :128]
        ref[at + 1:at + 2, :] = v[:, 128:]

    put(rowst, 0, rm)
    put(rowst, 2, rsm)

    def z_all(src, dst, k):
        def one(i):
            d = (8 + i // 2 + 1) - 2 * ((i // 2 + 1) * (i % 2))
            send(src, dst.at[z], k, dev(u, yl, (z + d) % 16, c))
        send(src, dst.at[z], k, dev(u, yl, (z + 8) % 16, c))
        each(14, one)
        dst[z] = src[...]

    def plane_all(src, dst, k):
        def one(i):
            q = (p + 1 + i) % 32
            send(src, dst.at[p], k, chip(q // 2, q % 2))
        each(31, one)
        dst[p] = src[...]

    def to_row(col):
        return jnp.broadcast_to(col, (SLOT, 128)).T[0:1, :]

    def to_cols(two):
        row = jnp.concatenate([two[0:1, :], two[1:2, :]], axis=1)
        half = jnp.broadcast_to(row, (128, SLOT)).T
        return jnp.concatenate([half, half], axis=1)

    z_all(rowst, rowb, ROWST)
    cm = jnp.max(logits, axis=1, keepdims=True)
    csm = jnp.sum(jnp.exp(logits - cm), axis=1, keepdims=True)
    put(colst, 0, to_row(cm))
    put(colst, 2, to_row(csm))
    plane_all(colst, colb, COLST)

    gather2(ct, Z_COT1, Z_COT2)
    tn[...] = ttv.T

    def totals(buf):
        v = buf[...]
        m = v[:, 0:2, :]
        top = jnp.max(m, axis=0)
        total = jnp.sum(v[:, 2:4, :] * jnp.exp(m - top[None]), axis=0)
        return top, total

    def core_swap(buf, xbuf, k):
        send(buf.at[1 - c], xbuf, k, dev(u, yl, z, 1 - c))

    def store_halves(buf, v):
        n = v.shape[0]
        for h in range(2):
            buf[h] = v[:, h * HALF:(h + 1) * HALF].astype(BF).reshape(n // 16, 16, HALF)

    wait_recv(colb.at[pl.ds(0, 31)], COLST)
    top, total = totals(colb)
    dv = jnp.exp(lt[...] - to_cols(top)) / to_cols(total)
    disp[...] = dv
    dispb[...] = dv.astype(BF)
    store_halves(pb.at[0], dot(dispb[...], tn[...]))
    core_swap(pb.at[0], xb.at[0], X_SI)

    wait_recv(rowb.at[pl.ds(0, 15)], ROWST)
    top, total = totals(rowb)
    topr = jnp.concatenate([top[0:1, :], top[1:2, :]], axis=1)
    totr = jnp.concatenate([total[0:1, :], total[1:2, :]], axis=1)
    cv = jnp.exp(lt[...] - topr) / totr
    combt[...] = cv
    combb[...] = cv.astype(BF)

    def rs32_send(j, kx, kr):
        wait_recv(xb.at[j], kx)
        sb[j] = (pb[j, c].astype(F32) + xb[j].astype(F32)).astype(BF)

        def one(i):
            q = (r + 1 + i) % 16
            send(sb.at[j, q], rb.at[j, r], kr, chip(q, c))
        each(15, one)
        rb[j, r] = sb[j, r]

    def rs32_sum(j, kr):
        wait_recv(rb.at[j, pl.ds(0, 15)], kr)
        return jnp.sum(rb[j].astype(F32), axis=0).astype(BF)

    def ag16_send(j, v, ka):
        ab[j, c, u] = v

        def one(i):
            q = (u + 1 + i) % 8
            send(ab.at[j, c, u], ab.at[j, c, u], ka, dev(q, yl, z, c))
        each(7, one)

    def ag16_forward(j, ka, kf):
        wait_recv(ab.at[j, 0, pl.ds(0, 7)], ka)
        send(ab.at[j, c], ab.at[j, c], kf, dev(u, yl, z, 1 - c))

    rs32_send(0, X_SI, R_SI)
    wait_recv(ct.at[:, pl.ds(0, 3)], Z_COT2)
    cn[...] = ct[...].reshape(D, TOK).T
    store_halves(pb.at[1], dot(combb[...], cn[...]))
    core_swap(pb.at[1], xb.at[1], X_DO)
    rs32_send(1, X_DO, R_DO)
    ag16_send(0, rs32_sum(0, R_SI), A_SI)
    ag16_forward(0, A_SI, F_SI)
    ag16_send(1, rs32_sum(1, R_DO), A_DO)

    def halves(j):
        return [ab[j, h].reshape(OWN, HALF) for h in range(2)]

    def rs16_send(j, kx, kr):
        wait_recv(xb2.at[j], kx)
        sb2[j] = (pb2[j, c].astype(F32) + xb2[j].astype(F32)).astype(BF)

        def one(i):
            q = (u + 1 + i) % 8
            send(sb2.at[j, q], rb2.at[j, u], kr, dev(q, yl, z, c))
        each(7, one)
        rb2[j, u] = sb2[j, u]

    def rs16_sum(j, kr):
        wait_recv(rb2.at[j, pl.ds(0, 7)], kr)
        return jnp.sum(rb2[j].astype(F32), axis=0).astype(BF)

    def ag32_send(j, v, ka):
        ab2[j, c, r] = v

        def one(i):
            q = (r + 1 + i) % 16
            send(ab2.at[j, c, r], ab2.at[j, c, r], ka, chip(q, c))
        each(15, one)

    def ag32_forward(j, ka, kf):
        wait_recv(ab2.at[j, 0, pl.ds(0, 15)], ka)
        send(ab2.at[j, c], ab2.at[j, c], kf, dev(u, yl, z, 1 - c))

    def rows(k):
        return slice(k * 64, (k + 1) * 64)

    wait_recv(ab.at[0, 0], F_SI)
    x0, x1 = halves(0)
    outs = []
    for k in range(2):
        pre = dot(x0[rows(k)], wi[k, :HALF, :]) + dot(x1[rows(k)], wi[k, HALF:, :])
        prev[k] = pre
        t = jnp.tanh(GELU_K * (pre + 0.044715 * (pre * pre * pre)))
        act = (0.5 * pre * (1.0 + t)).astype(BF)
        actv[k] = act
        outs.append(dot(act, wo[k]))
    store_halves(pb2.at[0], jnp.concatenate(outs, axis=0))
    core_swap(pb2.at[0], xb2.at[0], X_SO)

    ag16_forward(1, A_DO, F_DO)
    rs16_send(0, X_SO, R_SO)
    wait_recv(ab.at[1, 0], F_DO)
    g0, g1 = halves(1)
    outs = []
    for k in range(2):
        dact = dot(g0[rows(k)], wot[k, :HALF, :]) + dot(g1[rows(k)], wot[k, HALF:, :])
        pre = prev[k]
        sq = pre * pre
        t = jnp.tanh(GELU_K * (pre + 0.044715 * (sq * pre)))
        slope = 0.5 * (1.0 + t) + 0.5 * pre * (1.0 - t * t) * (GELU_K * (1.0 + 3.0 * 0.044715 * sq))
        dpre = (dact * slope).astype(BF)
        dprev[k] = dpre
        outs.append(dot(dpre, wit[k]))
    store_halves(pb2.at[1], jnp.concatenate(outs, axis=0))
    core_swap(pb2.at[1], xb2.at[1], X_DI)
    rs16_send(1, X_DI, R_DI)
    ag32_send(0, rs16_sum(0, R_SO), A_SO)

    for k in range(2):
        xt0, xt1 = x0[rows(k)].T, x1[rows(k)].T
        gwi[k, :HALF, :] = dot(xt0, dprev[k]).astype(BF)
        gwi[k, HALF:, :] = dot(xt1, dprev[k]).astype(BF)
        at = actv[k].T
        gwo[k, :, :HALF] = dot(at, g0[rows(k)]).astype(BF)
        gwo[k, :, HALF:] = dot(at, g1[rows(k)]).astype(BF)
    local(gwi, gwin_o, L_GWI)
    local(gwo, gwout_o, L_GWO)

    ag32_send(1, rs16_sum(1, R_DI), A_DI)
    ag32_forward(0, A_SO, F_SO)
    ag32_forward(1, A_DI, F_DI)

    def full(j):
        return [ab2[j, h].reshape(SLOT, HALF) for h in range(2)]

    def scatter1(j, k):
        def to(step):
            return dev(u, yl, (z + step) % 16, c)
        send(pz.at[j, :, (zl + 1) % 4], rz.at[j, 0], k, to(1))
        send(pz.at[j, :, (zl + 3) % 4], rz.at[j, 1], k, to(15))
        send(pz.at[j, pl.ds(0, 2), (zl + 2) % 4], rz.at[j, 2, pl.ds(0, 2)], k, to(2))
        send(pz.at[j, pl.ds(2, 2), (zl + 2) % 4], rz.at[j, 2, pl.ds(2, 2)], k, to(14))

    def scatter2(j, k1, k2):
        wait_recv(rz.at[j], k1)
        v = pz[j, :, zl].astype(F32)
        for i in range(3):
            v = v + rz[j, i].astype(F32)
        sz[j] = v.astype(BF)

        def one(i):
            zz = (zh + (i + 1) // 2) % 4
            yy = (yl + (i + 1) % 2) % 2
            send(sz.at[j, zz, yy], fz.at[j, zh, yl], k2, dev(u, yy, zz * 4 + zl, c))
        each(7, one)
        fz[j, zh, yl] = sz[j, zh, yl]

    def scatter3(j, k2, out, lk):
        wait_recv(seven, k2)
        v = jnp.sum(fz[j].astype(F32), axis=0).astype(BF)
        for h in range(2):
            outv[j, :, h * TOK:(h + 1) * TOK] = v[h]
        local(outv.at[j], out, lk)

    wait_recv(ab2.at[0, 0], F_SO)
    so0, so1 = full(0)
    ctv = ct[...].reshape(D, TOK)
    dcv = dot(so0, ctv[:HALF]) + dot(so1, ctv[HALF:])
    dcomb[...] = dcv
    put(rsum, 0, jnp.sum(combt[...] * dcv, axis=0, keepdims=True))
    z_all(rsum, rsumb, ROWSUM)

    wait_recv(ab2.at[1, 0], F_DI)
    di0, di1 = full(1)
    ddv = dot(di0, ttv[:HALF]) + dot(di1, ttv[HALF:])
    ddisp[...] = ddv
    put(csum, 0, to_row(jnp.sum(disp[...] * ddv, axis=1, keepdims=True)))
    plane_all(csum, csumb, COLSUM)

    pz[0, 0:2] = dot(so0.T, combb[...]).astype(BF).reshape(2, 4, 2, 32, TOK)
    pz[0, 2:4] = dot(so1.T, combb[...]).astype(BF).reshape(2, 4, 2, 32, TOK)
    scatter1(0, ZM1)
    part1[0:HALF, :] = dot(di0.T, dispb[...])
    part1[HALF:, :] = dot(di1.T, dispb[...])
    wait_recv(csumb.at[pl.ds(0, 31)], COLSUM)
    cols = to_cols(jnp.sum(csumb[...], axis=0))
    wait_recv(rsumb.at[pl.ds(0, 15)], ROWSUM)
    rtot = jnp.sum(rsumb[...], axis=0)
    rowr = jnp.concatenate([rtot[0:1, :], rtot[1:2, :]], axis=1)
    dlv = (disp[...] * (ddisp[...] - cols) + combt[...] * (dcomb[...] - rowr)).astype(BF)
    dlog[...] = dlv
    mfull = jnp.concatenate([mh[0], mh[1]], axis=1)
    pz[1] = (part1[...] + dot(mfull, dlv)).astype(BF).reshape(4, 4, 2, 32, TOK)
    scatter1(1, ZG1)
    store_halves(pb.at[2], dot(dlog[...], tn[...]))
    core_swap(pb.at[2], xb.at[2], X_GM)
    scatter2(0, ZM1, ZM2)
    rs32_send(2, X_GM, R_GM)
    scatter2(1, ZG1, ZG2)
    scatter3(0, ZM2, mixed_o, L_MX)
    ag16_send(2, rs32_sum(2, R_GM), A_GM)
    ag16_forward(2, A_GM, F_GM)
    wait_recv(ab.at[2, 0], F_GM)
    for h in range(2):
        gmv[h * HALF:(h + 1) * HALF, :] = ab[2, h].reshape(OWN, HALF).T
    local(gmv, gmix_o, L_GM)
    scatter3(1, ZG2, gtok_o, L_GT)

    for buf, k1, k2 in ((tt, Z_TOK1, Z_TOK2), (ct, Z_COT1, Z_COT2)):
        wait_send(seven, k1)
        wait_send(buf.at[:, pl.ds(0, 3)], k2)
    wait_send(mh.at[0], MIXX)
    wait_send(rowb.at[pl.ds(0, 15)], ROWST)
    wait_send(colb.at[pl.ds(0, 31)], COLST)
    wait_send(rsumb.at[pl.ds(0, 15)], ROWSUM)
    wait_send(csumb.at[pl.ds(0, 31)], COLSUM)
    for j, kx, kr, ka, kf in ((0, X_SI, R_SI, A_SI, F_SI), (1, X_DO, R_DO, A_DO, F_DO), (2, X_GM, R_GM, A_GM, F_GM)):
        wait_send(xb.at[j], kx)
        wait_send(rb.at[j, pl.ds(0, 15)], kr)
        wait_send(ab.at[j, 0, pl.ds(0, 7)], ka)
        wait_send(ab.at[j, 0], kf)
    for j, kx, kr, ka, kf in ((0, X_SO, R_SO, A_SO, F_SO), (1, X_DI, R_DI, A_DI, F_DI)):
        wait_send(xb2.at[j], kx)
        wait_send(rb2.at[j, pl.ds(0, 7)], kr)
        wait_send(ab2.at[j, 0, pl.ds(0, 15)], ka)
        wait_send(ab2.at[j, 0], kf)
    for j, k1, k2 in ((0, ZM1, ZM2), (1, ZG1, ZG2)):
        wait_send(rz.at[j], k1)
        wait_send(seven, k2)
    wait(gwi, ls.at[L_GWI])
    wait(gwo, ls.at[L_GWO])
    wait(outv.at[0], ls.at[L_MX])
    wait(outv.at[1], ls.at[L_GT])
    wait(gmv, ls.at[L_GM])


def per_device(tokens, mix, w_in, w_out, cotangent):
    scratch = [
        ((2, 32, TOK), BF), ((2, 32, TOK), BF),
        ((4, 4, 2, 32, TOK), BF), ((4, 4, 2, 32, TOK), BF),
        ((TOK, D), BF), ((TOK, D), BF),
        ((2, D, OWN), BF), ((SLOT, D), BF),
        ((2, D, HID), BF), ((2, HID, D), BF),
        ((2, HID, D), BF), ((2, D, HID), BF),
        ((8, 128), F32), ((8, 128), F32), ((16, 8, 128), F32), ((32, 8, 128), F32),
        ((8, 128), F32), ((8, 128), F32), ((16, 8, 128), F32), ((32, 8, 128), F32),
        ((3, 2, 16, 16, HALF), BF), ((3, 16, 16, HALF), BF), ((3, 16, 16, HALF), BF),
        ((3, 16, 16, HALF), BF), ((3, 2, 8, 16, HALF), BF),
        ((2, 2, 8, 16, HALF), BF), ((2, 8, 16, HALF), BF), ((2, 8, 16, HALF), BF),
        ((2, 8, 16, HALF), BF), ((2, 2, 16, 16, HALF), BF),
        ((2, 4, 4, 2, 32, TOK), BF), ((2, 3, 4, 2, 32, TOK), BF),
        ((2, 4, 2, 32, TOK), BF), ((2, 4, 2, 32, TOK), BF),
        ((SLOT, TOK), F32), ((SLOT, TOK), F32), ((SLOT, TOK), BF), ((SLOT, TOK), F32), ((SLOT, TOK), BF),
        ((SLOT, TOK), F32), ((SLOT, TOK), F32), ((SLOT, TOK), BF), ((D, TOK), F32),
        ((2, 64, HID), F32), ((2, 64, HID), BF), ((2, 64, HID), BF),
        ((2, D, HID), BF), ((2, HID, D), BF), ((2, 32, 2 * TOK), BF), ((D, OWN), BF),
        ((7, 32, TOK), BF),
    ]
    hbm = pl.BlockSpec(memory_space=pl.ANY)
    mixed_t, gtok_t, gmix, gwin, gwout = pl.pallas_call(
        kernel,
        out_shape=(
            jax.ShapeDtypeStruct((32, 512), BF),
            jax.ShapeDtypeStruct((32, 512), BF),
            jax.ShapeDtypeStruct(mix.shape, BF),
            jax.ShapeDtypeStruct(w_in.shape, BF),
            jax.ShapeDtypeStruct(w_out.shape, BF),
        ),
        in_specs=[hbm] * 5,
        out_specs=[hbm] * 5,
        scratch_shapes=[pltpu.VMEM(shape, kind) for shape, kind in scratch] + [
            pltpu.SemaphoreType.DMA((NSEM,)),
            pltpu.SemaphoreType.DMA((NSEM,)),
            pltpu.SemaphoreType.DMA((NLOC,)),
        ],
        compiler_params=pltpu.CompilerParams(
            collective_id=0, has_side_effects=True, vmem_limit_bytes=48 * 1024 * 1024
        ),
        name="soft_moe",
    )(tokens.T, mix, w_in, w_out, cotangent.T)
    return mixed_t.T, gtok_t.T, gmix, gwin, gwout


def solution(mesh):
    placed = (
        P("seq", "expert"),
        P(None, "expert"),
        P("expert", None, "seq"),
        P("expert", "seq", None),
        P("seq", "expert"),
    )
    return jax.shard_map(
        per_device,
        mesh=mesh,
        in_specs=placed,
        out_specs=(
            P("seq", "expert"),
            P("seq", "expert"),
            P(None, "expert"),
            P("expert", None, "seq"),
            P("expert", "seq", None),
        ),
        check_vma=False,
    )
```

```python
import functools
import math

import jax
import jax.numpy as jnp
from jax import lax
from jax.experimental import pallas as pl
from jax.experimental.pallas import tpu as pltpu
from jax.sharding import PartitionSpec as P

MESH = pl.DeviceIdType.MESH
F32 = jnp.float32
BF = jnp.bfloat16
GELU_K = math.sqrt(2.0 / math.pi)

D = 1024
TOK = 256
SLOT = 256
OWN = 128
HID = 256
HALF = 512

(TK_A, TK_B, TK_C, TK_D, CT_A, CT_B, CT_C, CT_D, ROWST, COLST, ROWSUM, COLSUM, MIXX,
 X_SI, R_SI, A_SI, X_DO, R_DO, A_DO, X_GM, R_GM, A_GM, R_SO, A_SO, F_SO, R_DI, A_DI, F_DI,
 MX_A, MX_B, MX_C, GT_A, GT_B, GT_C, NSEM) = range(35)
(L_TOK, L_COT, L_MIX, L_WI, L_WO, L_GWI, L_GWO, L_MX, L_GT, L_GM, NLOC) = range(11)


def dot(a, b):
    return jnp.dot(a, b, preferred_element_type=F32)


def kernel(tok_h, mix_h, win_h, wout_h, cot_h,
           mixed_o, gtok_o, gmix_o, gwin_o, gwout_o,
           tokv, cotv, tt, ct, tn, cn, mh, mt, wi, wo, wit, wot,
           rowst, colst, rowb, colb, rsum, csum, rsumb, csumb,
           pb, xb, sb, rb, ab, pb2, rb2, ab2,
           pz, rz, sz, fz, lt, disp, dispb, combt, combb, dcomb, ddisp, dlog, part1,
           prev, actv, dprev, gwi, gwo, outv, gmv, size,
           ss, rs, ls):
    s = lax.axis_index("seq")
    e = lax.axis_index("expert")
    u, c = s // 2, s % 2
    z, yl = e // 2, e % 2
    r = yl * 8 + u
    p = r * 2 + c

    def dev(u_, yl_, z_, c_):
        return (u_ * 2 + c_, z_ * 2 + yl_)

    def chip(r_, c_):
        return dev(r_ % 8, r_ // 8, z, c_)

    def send(src, dst, k, to, rk=None):
        sent[k] = 1
        pltpu.make_async_remote_copy(
            src_ref=src, dst_ref=dst, send_sem=ss.at[k], recv_sem=rs.at[k if rk is None else rk],
            device_id=to, device_id_type=MESH).start()

    def wait(ref, sem):
        pltpu.make_async_copy(ref, ref, sem).wait()

    sent, got = {}, set()

    def pieces(n):
        return size.at[pl.ds(0, n)]

    REFS = {MIXX: mh.at[0],
            ROWST: rowb.at[pl.ds(0, 15)], COLST: colb.at[pl.ds(0, 31)], ROWSUM: rsumb.at[pl.ds(0, 15)], COLSUM: csumb.at[pl.ds(0, 31)],
            MX_A: pieces(10), MX_B: pieces(8), MX_C: pieces(13), GT_A: pieces(10), GT_B: pieces(8), GT_C: pieces(13)}
    for ka, kb, kc, kd in ((TK_A, TK_B, TK_C, TK_D), (CT_A, CT_B, CT_C, CT_D)):
        REFS.update({ka: pieces(2), kb: pieces(2), kc: pieces(9), kd: pieces(18)})
    for j, kx, kr, ka in ((0, X_SI, R_SI, A_SI), (1, X_DO, R_DO, A_DO), (2, X_GM, R_GM, A_GM)):
        REFS.update({kx: xb.at[j], kr: rb.at[j, pl.ds(0, 15)], ka: rb.at[j, pl.ds(0, 15)]})
    for j, kr, ka, kf in ((0, R_SO, A_SO, F_SO), (1, R_DI, A_DI, F_DI)):
        REFS.update({kr: rb.at[j, pl.ds(0, 15)], ka: rb.at[j, pl.ds(0, 15)], kf: ab2.at[j, 0]})

    def wait_recv(k):
        got.add(k)
        wait(REFS[k], rs.at[k])

    def finish():
        for k in sent:
            if k not in got:
                wait(REFS[k], rs.at[k])
            wait(REFS[k], ss.at[k])

    def local(src, dst, k):
        cp = pltpu.make_async_copy(src, dst, ls.at[k])
        cp.start()
        return cp

    def each(n, f):
        def body(i, carry):
            f(i)
            return carry
        lax.fori_loop(0, n, body, 0)

    for h in range(2):
        local(tok_h.at[:, pl.ds(h * TOK, TOK)], tokv.at[h], L_TOK)
    for h in range(2):
        local(cot_h.at[:, pl.ds(h * TOK, TOK)], cotv.at[h], L_COT)
    local(mix_h, mh.at[yl], L_MIX)
    local(win_h, wi, L_WI)
    local(wout_h, wo, L_WO)

    bar = pltpu.get_barrier_semaphore()

    def sig(to):
        pl.semaphore_signal(bar, inc=1, device_id=to, device_id_type=MESH)

    def sig_plane(i):
        q = (p + 1 + i) % 32
        sig(chip(q // 2, q % 2))
    each(31, sig_plane)
    each(15, lambda i: sig(dev(u, yl, (z + 1 + i) % 16, c)))
    for o in (1, 15, 2, 14, 5, 11):
        sig(dev(u, 1 - yl, (z + o) % 16, c))
    pl.semaphore_wait(bar, 52)

    def zdev(o, yy):
        return dev(u, yy, (z + o) % 16, c)

    def gather1(src, dst, ka, kb, kc):
        for o, k in ((5, ka), (-5, kb), (1, kc), (-1, kc), (2, kc), (-2, kc)):
            for yy in range(2):
                send(src.at[yy], dst.at[z, yl], k, zdev(o + 16, yy))
        send(src.at[1 - yl], dst.at[z, yl], kc, zdev(0, 1 - yl))
        dst[z, yl] = src[yl]

    def gather2(buf, ka, kb, kd):
        wait_recv(ka)
        low = buf.at[(z + 11) % 16]
        for o in (3, 2, -2, 1, -1):
            send(low, low, kd, zdev(o + 16, yl))
        wait_recv(kb)
        high = buf.at[(z + 5) % 16]
        for o in (2, -2, 1, -1):
            send(high, high, kd, zdev(o + 16, yl))

    def gather3(kc, kd):
        wait_recv(kc)
        wait_recv(kd)

    wait(tokv, ls.at[L_TOK])
    gather1(tokv, tt, TK_A, TK_B, TK_C)
    wait(mh.at[0], ls.at[L_MIX])
    send(mh.at[yl], mh.at[yl], MIXX, dev(u, 1 - yl, z, c))
    mt[pl.ds(pl.multiple_of(yl * OWN, OWN), OWN), :] = mh[yl].T
    wait(cotv, ls.at[L_COT])
    gather2(tt, TK_A, TK_B, TK_D)
    gather1(cotv, ct, CT_A, CT_B, CT_C)
    wait_recv(MIXX)
    mt[pl.ds(pl.multiple_of((1 - yl) * OWN, OWN), OWN), :] = mh[1 - yl].T
    wait(wi, ls.at[L_WI])
    wait(wo, ls.at[L_WO])
    for k in range(2):
        wit[k] = wi[k].T
        wot[k] = wo[k].T
    gather3(TK_C, TK_D)

    ttv = tt[...].reshape(D, TOK)
    logits = dot(mt[...], ttv)
    lt[...] = logits
    rm = jnp.max(logits, axis=0, keepdims=True)
    rsm = jnp.sum(jnp.exp(logits - rm), axis=0, keepdims=True)

    def put(ref, at, v):
        ref[at:at + 1, :] = v[:, :128]
        ref[at + 1:at + 2, :] = v[:, 128:]

    put(rowst, 0, rm)
    put(rowst, 2, rsm)

    def z_all(src, dst, k):
        def one(i):
            d = (8 + i // 2 + 1) - 2 * ((i // 2 + 1) * (i % 2))
            send(src, dst.at[z], k, dev(u, yl, (z + d) % 16, c))
        send(src, dst.at[z], k, dev(u, yl, (z + 8) % 16, c))
        each(14, one)
        dst[z] = src[...]

    def plane_all(src, dst, k):
        def one(i):
            q = (p + 1 + i) % 32
            send(src, dst.at[p], k, chip(q // 2, q % 2))
        each(31, one)
        dst[p] = src[...]

    def to_row(col):
        return jnp.broadcast_to(col, (SLOT, 128)).T[0:1, :]

    def to_cols(two):
        row = jnp.concatenate([two[0:1, :], two[1:2, :]], axis=1)
        half = jnp.broadcast_to(row, (128, SLOT)).T
        return jnp.concatenate([half, half], axis=1)

    z_all(rowst, rowb, ROWST)
    gather2(ct, CT_A, CT_B, CT_D)
    cm = jnp.max(logits, axis=1, keepdims=True)
    csm = jnp.sum(jnp.exp(logits - cm), axis=1, keepdims=True)
    put(colst, 0, to_row(cm))
    put(colst, 2, to_row(csm))
    plane_all(colst, colb, COLST)

    tn[...] = ttv.T

    def totals(buf):
        v = buf[...]
        m = v[:, 0:2, :]
        top = jnp.max(m, axis=0)
        total = jnp.sum(v[:, 2:4, :] * jnp.exp(m - top[None]), axis=0)
        return top, total

    def core_swap(buf, xbuf, k):
        send(buf.at[1 - c], xbuf, k, dev(u, yl, z, 1 - c))

    def store_halves(buf, v):
        n = v.shape[0]
        for h in range(2):
            buf[h] = v[:, h * HALF:(h + 1) * HALF].astype(BF).reshape(n // 16, 16, HALF)

    def rs32_send(j, kx, kr):
        wait_recv(kx)
        sb[j] = (pb[j, c].astype(F32) + xb[j].astype(F32)).astype(BF)

        def one(i):
            q = (r + 1 + i) % 16
            send(sb.at[j, q], rb.at[j, r], kr, chip(q, c))
        each(15, one)
        rb[j, r] = sb[j, r]

    def rs32_sum(j, kr):
        wait_recv(kr)
        return jnp.sum(rb[j].astype(F32), axis=0).astype(BF)

    me = u * 2 + c

    def mate(i):
        q = (me + 1 + i) % 16
        return q // 2, q % 2

    def ag16_send(j, v, ka):
        ab[j, c, u] = v

        def one(i):
            qu, qc = mate(i)
            send(ab.at[j, c, u], ab.at[j, c, u], ka, dev(qu, yl, z, qc))
        each(15, one)

    wait_recv(COLST)
    top, total = totals(colb)
    dv = jnp.exp(lt[...] - to_cols(top)) / to_cols(total)
    disp[...] = dv
    dispb[...] = dv.astype(BF)
    store_halves(pb.at[0], dot(dispb[...], tn[...]))
    core_swap(pb.at[0], xb.at[0], X_SI)
    gather3(CT_C, CT_D)
    cn[...] = ct[...].reshape(D, TOK).T
    rs32_send(0, X_SI, R_SI)

    wait_recv(ROWST)
    top, total = totals(rowb)
    topr = jnp.concatenate([top[0:1, :], top[1:2, :]], axis=1)
    totr = jnp.concatenate([total[0:1, :], total[1:2, :]], axis=1)
    cv = jnp.exp(lt[...] - topr) / totr
    combt[...] = cv
    combb[...] = cv.astype(BF)
    store_halves(pb.at[1], dot(combb[...], cn[...]))
    core_swap(pb.at[1], xb.at[1], X_DO)
    rs32_send(1, X_DO, R_DO)
    ag16_send(0, rs32_sum(0, R_SI), A_SI)
    ag16_send(1, rs32_sum(1, R_DO), A_DO)

    def halves(j):
        return [ab[j, h].reshape(OWN, HALF) for h in range(2)]

    def rs16_send(j, v, kr):
        store_halves(pb2.at[j], v)

        def one(i):
            qu, qc = mate(i)
            send(pb2.at[j, qc, qu], rb2.at[j, me], kr, dev(qu, yl, z, qc))
        each(15, one)
        rb2[j, me] = pb2[j, c, u]

    def rs16_sum(j, kr):
        wait_recv(kr)
        return jnp.sum(rb2[j].astype(F32), axis=0).astype(BF)

    def ag32_send(j, v, ka):
        ab2[j, c, r] = v

        def one(i):
            q = (r + 1 + i) % 16
            send(ab2.at[j, c, r], ab2.at[j, c, r], ka, chip(q, c))
        each(15, one)

    def ag32_forward(j, ka, kf):
        wait_recv(ka)
        send(ab2.at[j, c], ab2.at[j, c], kf, dev(u, yl, z, 1 - c))

    def rows(k):
        return slice(k * 64, (k + 1) * 64)

    wait_recv(A_SI)
    x0, x1 = halves(0)
    outs = []
    for k in range(2):
        pre = dot(x0[rows(k)], wi[k, :HALF, :]) + dot(x1[rows(k)], wi[k, HALF:, :])
        prev[k] = pre
        t = jnp.tanh(GELU_K * (pre + 0.044715 * (pre * pre * pre)))
        act = (0.5 * pre * (1.0 + t)).astype(BF)
        actv[k] = act
        outs.append(dot(act, wo[k]))
    rs16_send(0, jnp.concatenate(outs, axis=0), R_SO)

    wait_recv(A_DO)
    g0, g1 = halves(1)
    outs = []
    for k in range(2):
        dact = dot(g0[rows(k)], wot[k, :HALF, :]) + dot(g1[rows(k)], wot[k, HALF:, :])
        pre = prev[k]
        sq = pre * pre
        t = jnp.tanh(GELU_K * (pre + 0.044715 * (sq * pre)))
        slope = 0.5 * (1.0 + t) + 0.5 * pre * (1.0 - t * t) * (GELU_K * (1.0 + 3.0 * 0.044715 * sq))
        dpre = (dact * slope).astype(BF)
        dprev[k] = dpre
        outs.append(dot(dpre, wit[k]))
    rs16_send(1, jnp.concatenate(outs, axis=0), R_DI)
    ag32_send(0, rs16_sum(0, R_SO), A_SO)

    for k in range(2):
        xt0, xt1 = x0[rows(k)].T, x1[rows(k)].T
        gwi[k, :HALF, :] = dot(xt0, dprev[k]).astype(BF)
        gwi[k, HALF:, :] = dot(xt1, dprev[k]).astype(BF)
        at = actv[k].T
        gwo[k, :, :HALF] = dot(at, g0[rows(k)]).astype(BF)
        gwo[k, :, HALF:] = dot(at, g1[rows(k)]).astype(BF)
    local(gwi, gwin_o, L_GWI)
    local(gwo, gwout_o, L_GWO)

    ag32_send(1, rs16_sum(1, R_DI), A_DI)
    ag32_forward(0, A_SO, F_SO)

    def full(j):
        return [ab2[j, h].reshape(SLOT, HALF) for h in range(2)]

    def scatter1(j, ka, kb, kc):
        src = pz.at[j]

        def at(o):
            return (z + o + 16) % 16
        for i, o in enumerate((2, -2, 1, -1)):
            if i == 0:
                send(src.at[at(8)], rz.at[j, 0, 4], ka, zdev(3, yl))
            send(src.at[at(o + 5)], rz.at[j, 0, i], ka, zdev(o + 16, yl))
            send(src.at[at(o - 5)], rz.at[j, 1, i], kb, zdev(o + 16, yl))
        for i, o in enumerate((2, -2, 1, -1)):
            for yy in range(2):
                send(src.at[at(o), yy], fz.at[j, 1 + i, yl], kc, zdev(o + 16, yy))
        send(src.at[z, 1 - yl], fz.at[j, 0, yl], kc, zdev(0, 1 - yl))

    def scatter2(j, ka, kb, kc):
        for h, k, o, n in ((0, ka, 5, 5), (1, kb, -5, 4)):
            wait_recv(k)
            v = pz[j, (z + o + 16) % 16].astype(F32)
            for i in range(n):
                v = v + rz[j, h, i].astype(F32)
            sz[j, h] = v.astype(BF)
            for yy in range(2):
                send(sz.at[j, h, yy], fz.at[j, 5 + h, yl], kc, zdev(o + 16, yy))
        fz[j, 0, yl] = pz[j, z, yl]

    def scatter3(j, k2, out, lk):
        wait_recv(k2)
        v = jnp.sum(fz[j].astype(F32), axis=0).astype(BF)
        for h in range(2):
            outv[j, :, h * TOK:(h + 1) * TOK] = v[h]
        local(outv.at[j], out, lk)

    wait_recv(F_SO)
    so0, so1 = full(0)
    ctv = ct[...].reshape(D, TOK)
    dcv = dot(so0, ctv[:HALF]) + dot(so1, ctv[HALF:])
    dcomb[...] = dcv
    put(rsum, 0, jnp.sum(combt[...] * dcv, axis=0, keepdims=True))
    z_all(rsum, rsumb, ROWSUM)
    ag32_forward(1, A_DI, F_DI)
    pz[0, 0:8] = dot(so0.T, combb[...]).astype(BF).reshape(8, 2, 32, TOK)
    pz[0, 8:16] = dot(so1.T, combb[...]).astype(BF).reshape(8, 2, 32, TOK)
    scatter1(0, MX_A, MX_B, MX_C)

    wait_recv(F_DI)
    di0, di1 = full(1)
    ddv = dot(di0, ttv[:HALF]) + dot(di1, ttv[HALF:])
    ddisp[...] = ddv
    put(csum, 0, to_row(jnp.sum(disp[...] * ddv, axis=1, keepdims=True)))
    plane_all(csum, csumb, COLSUM)

    part1[0:HALF, :] = dot(di0.T, dispb[...])
    part1[HALF:, :] = dot(di1.T, dispb[...])
    wait_recv(COLSUM)
    cols = to_cols(jnp.sum(csumb[...], axis=0))
    wait_recv(ROWSUM)
    rtot = jnp.sum(rsumb[...], axis=0)
    rowr = jnp.concatenate([rtot[0:1, :], rtot[1:2, :]], axis=1)
    dlv = (disp[...] * (ddisp[...] - cols) + combt[...] * (dcomb[...] - rowr)).astype(BF)
    dlog[...] = dlv
    store_halves(pb.at[2], dot(dlog[...], tn[...]))
    core_swap(pb.at[2], xb.at[2], X_GM)
    mfull = jnp.concatenate([mh[0], mh[1]], axis=1)
    pz[1] = (part1[...] + dot(mfull, dlv)).astype(BF).reshape(16, 2, 32, TOK)
    scatter1(1, GT_A, GT_B, GT_C)
    rs32_send(2, X_GM, R_GM)
    scatter2(0, MX_A, MX_B, MX_C)
    scatter2(1, GT_A, GT_B, GT_C)
    ag16_send(2, rs32_sum(2, R_GM), A_GM)
    scatter3(0, MX_C, mixed_o, L_MX)
    scatter3(1, GT_C, gtok_o, L_GT)
    wait_recv(A_GM)
    for h in range(2):
        gmv[h * HALF:(h + 1) * HALF, :] = ab[2, h].reshape(OWN, HALF).T
    local(gmv, gmix_o, L_GM)

    finish()
    wait(gwi, ls.at[L_GWI])
    wait(gwo, ls.at[L_GWO])
    wait(outv.at[0], ls.at[L_MX])
    wait(outv.at[1], ls.at[L_GT])
    wait(gmv, ls.at[L_GM])


def write_out(*refs):
    n = 5
    src, dst, held = refs[:n], refs[n:2 * n], refs[2 * n:3 * n]
    sem = refs[3 * n]
    loads = [pltpu.make_async_copy(src[i], held[i], sem.at[0, i]) for i in range(n)]
    stores = [pltpu.make_async_copy(held[i], dst[i], sem.at[1, i]) for i in range(n)]
    for cp in loads:
        cp.start()
    for i in range(n):
        loads[i].wait()
        stores[i].start()
    for cp in stores:
        cp.wait()


def per_device(tokens, mix, w_in, w_out, cotangent):
    scratch = [
        ((2, 32, TOK), BF), ((2, 32, TOK), BF),
        ((16, 2, 32, TOK), BF), ((16, 2, 32, TOK), BF),
        ((TOK, D), BF), ((TOK, D), BF),
        ((2, D, OWN), BF), ((SLOT, D), BF),
        ((2, D, HID), BF), ((2, HID, D), BF),
        ((2, HID, D), BF), ((2, D, HID), BF),
        ((8, 128), F32), ((8, 128), F32), ((16, 8, 128), F32), ((32, 8, 128), F32),
        ((8, 128), F32), ((8, 128), F32), ((16, 8, 128), F32), ((32, 8, 128), F32),
        ((3, 2, 16, 16, HALF), BF), ((3, 16, 16, HALF), BF), ((3, 16, 16, HALF), BF),
        ((3, 16, 16, HALF), BF), ((3, 2, 8, 16, HALF), BF),
        ((2, 2, 8, 16, HALF), BF), ((2, 16, 16, HALF), BF), ((2, 2, 16, 16, HALF), BF),
        ((2, 16, 2, 32, TOK), BF), ((2, 2, 5, 2, 32, TOK), BF),
        ((2, 2, 2, 32, TOK), BF), ((2, 7, 2, 32, TOK), BF),
        ((SLOT, TOK), F32), ((SLOT, TOK), F32), ((SLOT, TOK), BF), ((SLOT, TOK), F32), ((SLOT, TOK), BF),
        ((SLOT, TOK), F32), ((SLOT, TOK), F32), ((SLOT, TOK), BF), ((D, TOK), F32),
        ((2, 64, HID), F32), ((2, 64, HID), BF), ((2, 64, HID), BF),
        ((2, D, HID), BF), ((2, HID, D), BF), ((2, 32, 2 * TOK), BF), ((D, OWN), BF),
        ((18, 32, TOK), BF),
    ]
    hbm = pl.BlockSpec(memory_space=pl.ANY)
    results = pl.pallas_call(
        kernel,
        out_shape=(
            jax.ShapeDtypeStruct((32, 512), BF),
            jax.ShapeDtypeStruct((32, 512), BF),
            jax.ShapeDtypeStruct(mix.shape, BF),
            jax.ShapeDtypeStruct(w_in.shape, BF),
            jax.ShapeDtypeStruct(w_out.shape, BF),
        ),
        in_specs=[hbm] * 5,
        out_specs=[hbm] * 5,
        scratch_shapes=[pltpu.VMEM(shape, kind) for shape, kind in scratch] + [
            pltpu.SemaphoreType.DMA((NSEM,)),
            pltpu.SemaphoreType.DMA((NSEM,)),
            pltpu.SemaphoreType.DMA((NLOC,)),
        ],
        compiler_params=pltpu.CompilerParams(
            collective_id=0, has_side_effects=True, vmem_limit_bytes=63 * 1024 * 1024
        ),
        name="soft_moe",
    )(tokens.T, mix, w_in, w_out, cotangent.T)
    mixed_t, gtok_t, gmix, gwin, gwout = pl.pallas_call(
        write_out,
        out_shape=tuple(jax.ShapeDtypeStruct(v.shape, v.dtype) for v in results),
        in_specs=[hbm] * 5,
        out_specs=tuple([hbm] * 5),
        scratch_shapes=[pltpu.VMEM(v.shape, v.dtype) for v in results] + [pltpu.SemaphoreType.DMA((2, 5))],
        compiler_params=pltpu.CompilerParams(vmem_limit_bytes=63 * 1024 * 1024),
        name="write_out",
    )(*results)
    return mixed_t.T, gtok_t.T, gmix, gwin, gwout


def solution(mesh):
    placed = (
        P("seq", "expert"),
        P(None, "expert"),
        P("expert", None, "seq"),
        P("expert", "seq", None),
        P("seq", "expert"),
    )
    return jax.shard_map(
        per_device,
        mesh=mesh,
        in_specs=placed,
        out_specs=(
            P("seq", "expert"),
            P("seq", "expert"),
            P(None, "expert"),
            P("expert", None, "seq"),
            P("expert", "seq", None),
        ),
        check_vma=False,
    )
```

```python
import functools
import math

import jax
import jax.numpy as jnp
from jax import lax
from jax.experimental import pallas as pl
from jax.experimental.pallas import tpu as pltpu
from jax.sharding import PartitionSpec as P

MESH = pl.DeviceIdType.MESH
F32 = jnp.float32
BF = jnp.bfloat16
GELU_K = math.sqrt(2.0 / math.pi)

D = 1024
TOK = 256
SLOT = 256
OWN = 128
HID = 256
HALF = 512

(TK_A, TK_B, TK_C, TK_D, CT_A, CT_B, CT_C, CT_D, ROWST, COLST, ROWSUM, COLSUM, MIXX,
 X_SI, R_SI, A_SI, X_DO, R_DO, A_DO, X_GM, R_GM, A_GM, R_SO, A_SO, F_SO, R_DI, A_DI, F_DI,
 MX_A, MX_B, MX_C, GT_A, GT_B, GT_C, NSEM) = range(35)
(L_TOK, L_COT, L_MIX, L_WI, L_WO, L_GWI, L_GWO, L_MX, L_GT, L_GM, NLOC) = range(11)


def dot(a, b):
    return jnp.dot(a, b, preferred_element_type=F32)


def kernel(tok_h, mix_h, win_h, wout_h, cot_h,
           mixed_o, gtok_o, gmix_o, gwin_o, gwout_o,
           tokv, cotv, tt, ct, tn, cn, mh, mt, wi, wo, wit, wot,
           rowst, colst, rowb, colb, rsum, csum, rsumb, csumb,
           pb, xb, sb, rb, ab, pb2, rb2, ab2,
           pz, rz, sz, fz, lt, disp, dispb, combt, combb, dcomb, ddisp, dlog, part1,
           prev, actv, dprev, gwi, gwo, outv, gmv, size,
           ss, rs, ls):
    s = lax.axis_index("seq")
    e = lax.axis_index("expert")
    u, c = s // 2, s % 2
    z, yl = e // 2, e % 2
    r = yl * 8 + u
    p = s * 2 + yl
    flip_s = [2 ** k * (1 - 2 * ((s // 2 ** k) % 2)) for k in range(4)]
    flip_e = [2 ** k * (1 - 2 * ((e // 2 ** k) % 2)) for k in range(5)]
    flip_u = [2 ** k * (1 - 2 * ((u // 2 ** k) % 2)) for k in range(3)] + [8 * (1 - 2 * yl)]

    def flipped(v, weights, j):
        for k, w in enumerate(weights):
            if (j >> k) % 2:
                v = v + w
        return v

    def peer(j, b=0):
        return flipped(s, flip_s, j), flipped(e, flip_e, b)

    def dev(u_, yl_, z_, c_):
        return (u_ * 2 + c_, z_ * 2 + yl_)

    def send(src, dst, k, to, rk=None):
        sent[k] = 1
        pltpu.make_async_remote_copy(
            src_ref=src, dst_ref=dst, send_sem=ss.at[k], recv_sem=rs.at[k if rk is None else rk],
            device_id=to, device_id_type=MESH).start()

    def wait(ref, sem):
        pltpu.make_async_copy(ref, ref, sem).wait()

    sent, got = {}, set()

    def pieces(n):
        return size.at[pl.ds(0, n)]

    REFS = {MIXX: mh.at[0],
            ROWST: rowb.at[pl.ds(0, 15)], COLST: colb.at[pl.ds(0, 31)], ROWSUM: rsumb.at[pl.ds(0, 15)], COLSUM: csumb.at[pl.ds(0, 31)],
            MX_A: pieces(10), MX_B: pieces(8), MX_C: pieces(13), GT_A: pieces(10), GT_B: pieces(8), GT_C: pieces(13)}
    for ka, kb, kc, kd in ((TK_A, TK_B, TK_C, TK_D), (CT_A, CT_B, CT_C, CT_D)):
        REFS.update({ka: pieces(2), kb: pieces(2), kc: pieces(9), kd: pieces(18)})
    for j, kx, kr, ka in ((0, X_SI, R_SI, A_SI), (1, X_DO, R_DO, A_DO), (2, X_GM, R_GM, A_GM)):
        REFS.update({kx: xb.at[j], kr: rb.at[j, pl.ds(0, 15)], ka: rb.at[j, pl.ds(0, 15)]})
    for j, kr, ka, kf in ((0, R_SO, A_SO, F_SO), (1, R_DI, A_DI, F_DI)):
        REFS.update({kr: rb.at[j, pl.ds(0, 15)], ka: rb.at[j, pl.ds(0, 15)], kf: ab2.at[j, 0]})

    def wait_recv(k):
        got.add(k)
        wait(REFS[k], rs.at[k])

    def finish():
        for k in sent:
            if k not in got:
                wait(REFS[k], rs.at[k])
            wait(REFS[k], ss.at[k])

    def local(src, dst, k):
        cp = pltpu.make_async_copy(src, dst, ls.at[k])
        cp.start()
        return cp

    for h in range(2):
        local(tok_h.at[:, pl.ds(h * TOK, TOK)], tokv.at[h], L_TOK)
    for h in range(2):
        local(cot_h.at[:, pl.ds(h * TOK, TOK)], cotv.at[h], L_COT)
    local(mix_h, mh.at[yl], L_MIX)
    local(win_h, wi, L_WI)
    local(wout_h, wo, L_WO)

    bar = pltpu.get_barrier_semaphore()

    def sig(to):
        pl.semaphore_signal(bar, inc=1, device_id=to, device_id_type=MESH)

    for d in (8, 9, 7, 10, 6, 11, 5, 12, 4, 13, 3, 14, 2, 15, 1):
        sig(dev(u, yl, (z + d) % 16, c))
    for o in (1, 15, 2, 14, 5, 11):
        sig(dev(u, 1 - yl, (z + o) % 16, c))
    for i in range(31, 0, -1):
        sig(peer(i // 2, i % 2))
    pl.semaphore_wait(bar, 52)

    def zdev(o, yy):
        return dev(u, yy, (z + o) % 16, c)

    def gather1(src, dst, ka, kb, kc):
        for o, k in ((5, ka), (-5, kb), (1, kc), (-1, kc), (2, kc), (-2, kc)):
            for yy in range(2):
                send(src.at[yy], dst.at[z, yl], k, zdev(o + 16, yy))
        send(src.at[1 - yl], dst.at[z, yl], kc, zdev(0, 1 - yl))
        dst[z, yl] = src[yl]

    def gather2(buf, ka, kb, kd):
        wait_recv(ka)
        low = buf.at[(z + 11) % 16]
        for o in (3, 2, -2, 1, -1):
            send(low, low, kd, zdev(o + 16, yl))
        wait_recv(kb)
        high = buf.at[(z + 5) % 16]
        for o in (2, -2, 1, -1):
            send(high, high, kd, zdev(o + 16, yl))

    def gather3(kc, kd):
        wait_recv(kc)
        wait_recv(kd)

    wait(tokv, ls.at[L_TOK])
    gather1(tokv, tt, TK_A, TK_B, TK_C)
    wait(mh.at[0], ls.at[L_MIX])
    send(mh.at[yl], mh.at[yl], MIXX, dev(u, 1 - yl, z, c))
    mt[pl.ds(pl.multiple_of(yl * OWN, OWN), OWN), :] = mh[yl].T
    wait(cotv, ls.at[L_COT])
    gather2(tt, TK_A, TK_B, TK_D)
    gather1(cotv, ct, CT_A, CT_B, CT_C)
    wait_recv(MIXX)
    mt[pl.ds(pl.multiple_of((1 - yl) * OWN, OWN), OWN), :] = mh[1 - yl].T
    wait(wi, ls.at[L_WI])
    wait(wo, ls.at[L_WO])
    for k in range(2):
        wit[k] = wi[k].T
        wot[k] = wo[k].T
    gather3(TK_C, TK_D)

    ttv = tt[...].reshape(D, TOK)
    logits = dot(mt[...], ttv)
    lt[...] = logits
    rm = jnp.max(logits, axis=0, keepdims=True)
    rsm = jnp.sum(jnp.exp(logits - rm), axis=0, keepdims=True)

    def put(ref, at, v):
        ref[at:at + 1, :] = v[:, :128]
        ref[at + 1:at + 2, :] = v[:, 128:]

    put(rowst, 0, rm)
    put(rowst, 2, rsm)

    def z_all(src, dst, k):
        for d in (8, 9, 7, 10, 6, 11, 5, 12, 4, 13, 3, 14, 2, 15, 1):
            send(src, dst.at[z], k, zdev(d, yl))
        dst[z] = src[...]

    def plane_all(src, dst, k):
        for i in range(31, 0, -1):
            send(src, dst.at[p], k, peer(i // 2, i % 2))
        dst[p] = src[...]

    def to_row(col):
        return jnp.broadcast_to(col, (SLOT, 128)).T[0:1, :]

    def to_cols(two):
        row = jnp.concatenate([two[0:1, :], two[1:2, :]], axis=1)
        half = jnp.broadcast_to(row, (128, SLOT)).T
        return jnp.concatenate([half, half], axis=1)

    z_all(rowst, rowb, ROWST)
    cm = jnp.max(logits, axis=1, keepdims=True)
    csm = jnp.sum(jnp.exp(logits - cm), axis=1, keepdims=True)
    put(colst, 0, to_row(cm))
    put(colst, 2, to_row(csm))
    plane_all(colst, colb, COLST)
    gather2(ct, CT_A, CT_B, CT_D)

    tn[...] = ttv.T

    def totals(buf):
        v = buf[...]
        m = v[:, 0:2, :]
        top = jnp.max(m, axis=0)
        total = jnp.sum(v[:, 2:4, :] * jnp.exp(m - top[None]), axis=0)
        return top, total

    def core_swap(buf, xbuf, k):
        send(buf.at[1 - c], xbuf, k, dev(u, yl, z, 1 - c))

    def store_halves(buf, v):
        n = v.shape[0]
        for h in range(2):
            buf[h] = v[:, h * HALF:(h + 1) * HALF].astype(BF).reshape(n // 16, 16, HALF)

    def rs32_send(j, kx, kr):
        wait_recv(kx)
        sb[j] = (pb[j, c].astype(F32) + xb[j].astype(F32)).astype(BF)

        for i in range(15, 0, -1):
            send(sb.at[j, flipped(r, flip_u, i)], rb.at[j, r], kr, peer(2 * (i % 8), i // 8))
        rb[j, r] = sb[j, r]

    def rs32_sum(j, kr):
        wait_recv(kr)
        return jnp.sum(rb[j].astype(F32), axis=0).astype(BF)

    def ag16_send(j, v, ka):
        ab[j, c, u] = v
        for i in range(15, 0, -1):
            send(ab.at[j, c, u], ab.at[j, c, u], ka, peer(i))

    wait_recv(COLST)
    top, total = totals(colb)
    dv = jnp.exp(lt[...] - to_cols(top)) / to_cols(total)
    disp[...] = dv
    dispb[...] = dv.astype(BF)
    store_halves(pb.at[0], dot(dispb[...], tn[...]))
    core_swap(pb.at[0], xb.at[0], X_SI)
    gather3(CT_C, CT_D)
    cn[...] = ct[...].reshape(D, TOK).T
    rs32_send(0, X_SI, R_SI)

    wait_recv(ROWST)
    top, total = totals(rowb)
    topr = jnp.concatenate([top[0:1, :], top[1:2, :]], axis=1)
    totr = jnp.concatenate([total[0:1, :], total[1:2, :]], axis=1)
    cv = jnp.exp(lt[...] - topr) / totr
    combt[...] = cv
    combb[...] = cv.astype(BF)
    store_halves(pb.at[1], dot(combb[...], cn[...]))
    core_swap(pb.at[1], xb.at[1], X_DO)
    rs32_send(1, X_DO, R_DO)
    ag16_send(0, rs32_sum(0, R_SI), A_SI)
    ag16_send(1, rs32_sum(1, R_DO), A_DO)

    def halves(j):
        return [ab[j, h].reshape(OWN, HALF) for h in range(2)]

    def rs16_send(j, v, kr):
        store_halves(pb2.at[j], v)
        for i in range(15, 0, -1):
            qu, qc = flipped(u, flip_u, i // 2), flipped(c, flip_s[:1], i % 2)
            send(pb2.at[j, qc, qu], rb2.at[j, s], kr, peer(i))
        rb2[j, s] = pb2[j, c, u]

    def rs16_sum(j, kr):
        wait_recv(kr)
        return jnp.sum(rb2[j].astype(F32), axis=0).astype(BF)

    def ag32_send(j, v, ka):
        ab2[j, c, r] = v
        for i in range(15, 0, -1):
            send(ab2.at[j, c, r], ab2.at[j, c, r], ka, peer(2 * (i % 8), i // 8))

    def ag32_forward(j, ka, kf):
        wait_recv(ka)
        send(ab2.at[j, c], ab2.at[j, c], kf, dev(u, yl, z, 1 - c))

    def rows(k):
        return slice(k * 64, (k + 1) * 64)

    wait_recv(A_SI)
    x0, x1 = halves(0)
    outs = []
    for k in range(2):
        pre = dot(x0[rows(k)], wi[k, :HALF, :]) + dot(x1[rows(k)], wi[k, HALF:, :])
        prev[k] = pre
        t = jnp.tanh(GELU_K * (pre + 0.044715 * (pre * pre * pre)))
        act = (0.5 * pre * (1.0 + t)).astype(BF)
        actv[k] = act
        outs.append(dot(act, wo[k]))
    rs16_send(0, jnp.concatenate(outs, axis=0), R_SO)

    wait_recv(A_DO)
    g0, g1 = halves(1)
    outs = []
    for k in range(2):
        dact = dot(g0[rows(k)], wot[k, :HALF, :]) + dot(g1[rows(k)], wot[k, HALF:, :])
        pre = prev[k]
        sq = pre * pre
        t = jnp.tanh(GELU_K * (pre + 0.044715 * (sq * pre)))
        slope = 0.5 * (1.0 + t) + 0.5 * pre * (1.0 - t * t) * (GELU_K * (1.0 + 3.0 * 0.044715 * sq))
        dpre = (dact * slope).astype(BF)
        dprev[k] = dpre
        outs.append(dot(dpre, wit[k]))
    rs16_send(1, jnp.concatenate(outs, axis=0), R_DI)
    ag32_send(0, rs16_sum(0, R_SO), A_SO)

    for k in range(2):
        xt0, xt1 = x0[rows(k)].T, x1[rows(k)].T
        gwi[k, :HALF, :] = dot(xt0, dprev[k]).astype(BF)
        gwi[k, HALF:, :] = dot(xt1, dprev[k]).astype(BF)
        at = actv[k].T
        gwo[k, :, :HALF] = dot(at, g0[rows(k)]).astype(BF)
        gwo[k, :, HALF:] = dot(at, g1[rows(k)]).astype(BF)
    local(gwi, gwin_o, L_GWI)
    local(gwo, gwout_o, L_GWO)

    ag32_send(1, rs16_sum(1, R_DI), A_DI)
    ag32_forward(0, A_SO, F_SO)

    def full(j):
        return [ab2[j, h].reshape(SLOT, HALF) for h in range(2)]

    def scatter1(j, ka, kb, kc):
        src = pz.at[j]

        def at(o):
            return (z + o + 16) % 16
        for i, o in enumerate((2, -2, 1, -1)):
            if i == 0:
                send(src.at[at(8)], rz.at[j, 0, 4], ka, zdev(3, yl))
            send(src.at[at(o + 5)], rz.at[j, 0, i], ka, zdev(o + 16, yl))
            send(src.at[at(o - 5)], rz.at[j, 1, i], kb, zdev(o + 16, yl))
        for i, o in enumerate((2, -2, 1, -1)):
            for yy in range(2):
                send(src.at[at(o), yy], fz.at[j, 1 + i, yl], kc, zdev(o + 16, yy))
        send(src.at[z, 1 - yl], fz.at[j, 0, yl], kc, zdev(0, 1 - yl))

    def scatter2(j, ka, kb, kc):
        for h, k, o, n in ((0, ka, 5, 5), (1, kb, -5, 4)):
            wait_recv(k)
            v = pz[j, (z + o + 16) % 16].astype(F32)
            for i in range(n):
                v = v + rz[j, h, i].astype(F32)
            sz[j, h] = v.astype(BF)
            for yy in range(2):
                send(sz.at[j, h, yy], fz.at[j, 5 + h, yl], kc, zdev(o + 16, yy))
        fz[j, 0, yl] = pz[j, z, yl]

    def scatter3(j, k2, out, lk):
        wait_recv(k2)
        v = jnp.sum(fz[j].astype(F32), axis=0).astype(BF)
        for h in range(2):
            outv[j, :, h * TOK:(h + 1) * TOK] = v[h]
        local(outv.at[j], out, lk)

    def by_halves(j, kf, buf):
        def part(h):
            return dot(ab2[j, h].reshape(SLOT, HALF), buf[pl.ds(h * 8, 8)].reshape(HALF, TOK))
        v = part(c)
        wait_recv(kf)
        return v + part(1 - c)

    dcv = by_halves(0, F_SO, ct)
    so0, so1 = full(0)
    dcomb[...] = dcv
    put(rsum, 0, jnp.sum(combt[...] * dcv, axis=0, keepdims=True))
    z_all(rsum, rsumb, ROWSUM)
    ag32_forward(1, A_DI, F_DI)
    pz[0, 0:8] = dot(so0.T, combb[...]).astype(BF).reshape(8, 2, 32, TOK)
    pz[0, 8:16] = dot(so1.T, combb[...]).astype(BF).reshape(8, 2, 32, TOK)
    scatter1(0, MX_A, MX_B, MX_C)

    ddv = by_halves(1, F_DI, tt)
    di0, di1 = full(1)
    ddisp[...] = ddv
    put(csum, 0, to_row(jnp.sum(disp[...] * ddv, axis=1, keepdims=True)))
    plane_all(csum, csumb, COLSUM)

    part1[0:HALF, :] = dot(di0.T, dispb[...])
    part1[HALF:, :] = dot(di1.T, dispb[...])
    wait_recv(COLSUM)
    cols = to_cols(jnp.sum(csumb[...], axis=0))
    wait_recv(ROWSUM)
    rtot = jnp.sum(rsumb[...], axis=0)
    rowr = jnp.concatenate([rtot[0:1, :], rtot[1:2, :]], axis=1)
    dlv = (disp[...] * (ddisp[...] - cols) + combt[...] * (dcomb[...] - rowr)).astype(BF)
    dlog[...] = dlv
    store_halves(pb.at[2], dot(dlog[...], tn[...]))
    core_swap(pb.at[2], xb.at[2], X_GM)
    mfull = jnp.concatenate([mh[0], mh[1]], axis=1)
    pz[1] = (part1[...] + dot(mfull, dlv)).astype(BF).reshape(16, 2, 32, TOK)
    scatter1(1, GT_A, GT_B, GT_C)
    rs32_send(2, X_GM, R_GM)
    scatter2(0, MX_A, MX_B, MX_C)
    scatter2(1, GT_A, GT_B, GT_C)
    ag16_send(2, rs32_sum(2, R_GM), A_GM)
    scatter3(0, MX_C, mixed_o, L_MX)
    scatter3(1, GT_C, gtok_o, L_GT)
    wait_recv(A_GM)
    for h in range(2):
        gmv[h * HALF:(h + 1) * HALF, :] = ab[2, h].reshape(OWN, HALF).T
    local(gmv, gmix_o, L_GM)

    finish()
    wait(gwi, ls.at[L_GWI])
    wait(gwo, ls.at[L_GWO])
    wait(outv.at[0], ls.at[L_MX])
    wait(outv.at[1], ls.at[L_GT])
    wait(gmv, ls.at[L_GM])


def write_out(*refs):
    n = 5
    src, dst, held = refs[:n], refs[n:2 * n], refs[2 * n:3 * n]
    sem = refs[3 * n]
    loads = [pltpu.make_async_copy(src[i], held[i], sem.at[0, i]) for i in range(n)]
    stores = [pltpu.make_async_copy(held[i], dst[i], sem.at[1, i]) for i in range(n)]
    for cp in loads:
        cp.start()
    for i in range(n):
        loads[i].wait()
        stores[i].start()
    for cp in stores:
        cp.wait()


def per_device(tokens, mix, w_in, w_out, cotangent):
    scratch = [
        ((2, 32, TOK), BF), ((2, 32, TOK), BF),
        ((16, 2, 32, TOK), BF), ((16, 2, 32, TOK), BF),
        ((TOK, D), BF), ((TOK, D), BF),
        ((2, D, OWN), BF), ((SLOT, D), BF),
        ((2, D, HID), BF), ((2, HID, D), BF),
        ((2, HID, D), BF), ((2, D, HID), BF),
        ((8, 128), F32), ((8, 128), F32), ((16, 8, 128), F32), ((32, 8, 128), F32),
        ((8, 128), F32), ((8, 128), F32), ((16, 8, 128), F32), ((32, 8, 128), F32),
        ((3, 2, 16, 16, HALF), BF), ((3, 16, 16, HALF), BF), ((3, 16, 16, HALF), BF),
        ((3, 16, 16, HALF), BF), ((3, 2, 8, 16, HALF), BF),
        ((2, 2, 8, 16, HALF), BF), ((2, 16, 16, HALF), BF), ((2, 2, 16, 16, HALF), BF),
        ((2, 16, 2, 32, TOK), BF), ((2, 2, 5, 2, 32, TOK), BF),
        ((2, 2, 2, 32, TOK), BF), ((2, 7, 2, 32, TOK), BF),
        ((SLOT, TOK), F32), ((SLOT, TOK), F32), ((SLOT, TOK), BF), ((SLOT, TOK), F32), ((SLOT, TOK), BF),
        ((SLOT, TOK), F32), ((SLOT, TOK), F32), ((SLOT, TOK), BF), ((D, TOK), F32),
        ((2, 64, HID), F32), ((2, 64, HID), BF), ((2, 64, HID), BF),
        ((2, D, HID), BF), ((2, HID, D), BF), ((2, 32, 2 * TOK), BF), ((D, OWN), BF),
        ((18, 32, TOK), BF),
    ]
    hbm = pl.BlockSpec(memory_space=pl.ANY)
    results = pl.pallas_call(
        kernel,
        out_shape=(
            jax.ShapeDtypeStruct((32, 512), BF),
            jax.ShapeDtypeStruct((32, 512), BF),
            jax.ShapeDtypeStruct(mix.shape, BF),
            jax.ShapeDtypeStruct(w_in.shape, BF),
            jax.ShapeDtypeStruct(w_out.shape, BF),
        ),
        in_specs=[hbm] * 5,
        out_specs=[hbm] * 5,
        scratch_shapes=[pltpu.VMEM(shape, kind) for shape, kind in scratch] + [
            pltpu.SemaphoreType.DMA((NSEM,)),
            pltpu.SemaphoreType.DMA((NSEM,)),
            pltpu.SemaphoreType.DMA((NLOC,)),
        ],
        compiler_params=pltpu.CompilerParams(
            collective_id=0, has_side_effects=True, vmem_limit_bytes=63 * 1024 * 1024
        ),
        name="soft_moe",
    )(tokens.T, mix, w_in, w_out, cotangent.T)
    mixed_t, gtok_t, gmix, gwin, gwout = pl.pallas_call(
        write_out,
        out_shape=tuple(jax.ShapeDtypeStruct(v.shape, v.dtype) for v in results),
        in_specs=[hbm] * 5,
        out_specs=tuple([hbm] * 5),
        scratch_shapes=[pltpu.VMEM(v.shape, v.dtype) for v in results] + [pltpu.SemaphoreType.DMA((2, 5))],
        compiler_params=pltpu.CompilerParams(vmem_limit_bytes=63 * 1024 * 1024),
        name="write_out",
    )(*results)
    return mixed_t.T, gtok_t.T, gmix, gwin, gwout


def solution(mesh):
    placed = (
        P("seq", "expert"),
        P(None, "expert"),
        P("expert", None, "seq"),
        P("expert", "seq", None),
        P("seq", "expert"),
    )
    return jax.shard_map(
        per_device,
        mesh=mesh,
        in_specs=placed,
        out_specs=(
            P("seq", "expert"),
            P("seq", "expert"),
            P(None, "expert"),
            P("expert", None, "seq"),
            P("expert", "seq", None),
        ),
        check_vma=False,
    )
```
